32 devices in a mesh: modes: 8 (over z, y), gy: 4 (over x, core).
Axes of the slice: x: 2, y: 2, z: 4, core: 2. Of those that a mesh axis runs over, the one named last changes fastest.
Arguments:
- forcing: float32 [768, 16384], P('gy', 'modes'), may hold values from -6 to 6
- wavenumbers: int32 [2, 16384], P(None, 'modes'), may hold values from 0 to 7
- eigvec: float32 [4, 36864], P('gy', 'modes'), may hold values from -1 to 1, as said below
- decay: float32 [768], P('gy'), may hold values from 0.1 to 10
Outputs:
- velocity: float32 [768, 16384], P('gy', 'modes')
The draws below stay inside these ranges and needn't reach their ends.
Inputs may be any that keep to these rules, and one draw needn't show every extreme that they name: `eigvec`: each row is an orthogonal 192 x 192 matrix stored row by row.
All inputs are finite; a program needn't handle non-finite values.
Results may differ from the reference program's by a relative error of at most 0.00027.
Values sent between devices are 32-bit elements; how exact they have to be, the bound alone decides.
A program may use at most 64 MiB of HBM per device.

```python
import math
import jax
import jax.numpy as jnp
from jax import lax

NB = 192
LINES = 16384
NY = 768


def block_basis(sub, margin):
    highest = lax.Precision.HIGHEST
    width = NB
    k_inner, k_rest, k_rates, k_order = jax.random.split(sub, 4)
    index = jnp.arange(width)
    first = (index == 0).astype(jnp.float32)
    last = (index == width - 1).astype(jnp.float32)
    inside = 1.0 - first - last
    inner = jax.random.normal(k_inner, (width, 2), jnp.float32) * inside[:, None]
    inner_basis, inner_upper = jnp.linalg.qr(inner)
    edge = math.sqrt(0.4)
    spread = math.sqrt(0.2)
    even = edge * (first + last) + spread * inner_basis[:, 0]
    odd = edge * (first - last) + spread * inner_basis[:, 1]
    paired = jnp.stack([even, odd], axis=1)
    raw = jax.random.normal(k_rest, (width, width - 2), jnp.float32)
    raw = raw - jnp.dot(paired, jnp.dot(paired.T, raw, precision=highest), precision=highest)
    raw = raw - jnp.dot(paired, jnp.dot(paired.T, raw, precision=highest), precision=highest)
    remainder, rest_upper = jnp.linalg.qr(raw)
    rest_rates = jnp.exp(jax.random.uniform(k_rates, (width - 2,), jnp.float32, 0.0, math.log(10.0)))
    rest_weight = 1.0 / rest_rates
    r_ss = jnp.sum(remainder[0] * remainder[0] * rest_weight)
    r_ee = jnp.sum(remainder[width - 1] * remainder[width - 1] * rest_weight)
    r_se = jnp.sum(remainder[0] * remainder[width - 1] * rest_weight)
    level = 2.0 + margin
    h_target = 4.0 * level / (level * level - 1.0)
    g_target = 4.0 / (level * level - 1.0)
    total = (h_target - 0.5 * (r_ss + r_ee)) / 0.4
    differ = (g_target - r_se) / 0.4
    w_even = 0.5 * (total + differ)
    w_odd = 0.5 * (total - differ)
    rates = jnp.concatenate([jnp.stack([1.0 / w_even, 1.0 / w_odd]), rest_rates])
    basis = jnp.concatenate([paired, remainder], axis=1)
    order = jax.random.permutation(k_order, width)
    return (basis[:, order].reshape(width * width), rates[order])


def blocks_draw(key):
    groups = NY // NB
    base = jax.random.fold_in(key, 17)
    keys = jax.random.split(base, groups)
    margin = 0.02
    return jax.vmap(lambda sub: block_basis(sub, margin))(keys)


def draw_eigvec(key, part):
    basis, rates = blocks_draw(key)
    return basis.astype(jnp.float32)


def draw_decay(key, part):
    basis, rates = blocks_draw(key)
    return rates.reshape(NY).astype(jnp.float32)


def plant(entries, stream_key, low, high):
    shape = entries.shape
    spot = [jax.random.randint(jax.random.fold_in(stream_key, axis), (), 0, shape[axis]) for axis in range(len(shape))]
    entries = entries.at[tuple(spot)].set(low)
    longest = shape.index(max(shape))
    spot[longest] = (spot[longest] + 1) % shape[longest]
    return entries.at[tuple(spot)].set(high)


def shard_levels(stream_key, shape, cuts, least, largest):
    gain = 1.0
    for axis_at, shards_of in cuts:
        steps = jax.random.uniform(jax.random.fold_in(jax.random.fold_in(stream_key, 6), axis_at), (shards_of,), jnp.float32, least / len(cuts), largest / len(cuts))
        gain = gain * jnp.repeat(jnp.exp(steps), shape[axis_at] // shards_of).reshape((-1,) + (1,) * (len(shape) - 1 - axis_at))
    return gain


def centred(key, dims, deviation, reach, cuts=(), kind=jnp.bfloat16):
    drawn = jax.random.normal(key, dims, jnp.float32) * deviation
    if len(cuts) > 0:
        drawn = shard_levels(key, dims, cuts, -0.22, 0.18) * drawn
    return jnp.clip(drawn, min=-reach, max=reach).astype(kind)


def setup_inputs(seed: int = 0) -> dict:
    key_of = jax.random.split(jax.random.key(seed), 5)
    return {
        "forcing": centred(key_of[0], (NY, LINES), 1.0, 6.0, ((0, 4), (1, 8)), jnp.float32),
        "wavenumbers": plant(jax.random.randint(key_of[1], (2, LINES), 0, 8), jax.random.fold_in(key_of[1], 1), 0, 7).astype(jnp.int32),
        "eigvec": draw_eigvec(jax.random.fold_in(key_of[4], 71), 0),
        "decay": draw_decay(jax.random.fold_in(key_of[4], 71), 0),
    }


coupling = 0.25

def reference(forcing, wavenumbers, eigvec, decay):
    highest = lax.Precision.HIGHEST
    kx = wavenumbers[0].astype(jnp.float32) / 64.0
    kz = wavenumbers[1].astype(jnp.float32) / 24.0
    shifts = kx * kx + kz * kz
    groups = NY // NB
    pieces = []
    for block in range(groups):
        matrix = eigvec[block].reshape(NB, NB)
        rates = decay[block * NB:(block + 1) * NB]
        rhs = forcing[block * NB:(block + 1) * NB]
        weight = 1.0 / (shifts[None, :] + rates[:, None])
        trans = jnp.dot(matrix.T, rhs, precision=highest)
        first_row = matrix[0]
        last_row = matrix[NB - 1]
        scaled = weight * trans
        p_start = jnp.dot(first_row, scaled, precision=highest)
        p_end = jnp.dot(last_row, scaled, precision=highest)
        g_ss = jnp.dot(first_row * first_row, weight, precision=highest)
        g_se = jnp.dot(first_row * last_row, weight, precision=highest)
        g_ee = jnp.dot(last_row * last_row, weight, precision=highest)
        pieces.append((matrix, weight, trans, p_start, p_end, g_ss, g_se, g_ee))
    q_prev = jnp.zeros(shifts.shape, jnp.float32)
    y_prev = jnp.zeros(shifts.shape, jnp.float32)
    states = []
    for block in range(groups):
        matrix, weight, trans, p_start, p_end, g_ss, g_se, g_ee = pieces[block]
        denom = 1.0 - coupling * g_ss * q_prev
        zero_part = (p_start - coupling * g_ss * y_prev) / denom
        one_part = p_end - coupling * g_se * y_prev + coupling * g_se * q_prev * zero_part
        q_zero = coupling * g_se / denom
        q_one = coupling * g_ee + coupling * g_se * q_prev * q_zero
        states.append((zero_part, one_part, q_zero, q_one))
        q_prev, y_prev = (q_one, one_part)
    a_next = jnp.zeros(shifts.shape, jnp.float32)
    starts = [None] * groups
    ends = [None] * groups
    for block in range(groups - 1, -1, -1):
        zero_part, one_part, q_zero, q_one = states[block]
        starts[block] = a_next
        ends[block] = one_part - q_one * a_next
        a_next = zero_part - q_zero * a_next
    outputs = []
    b_prev = jnp.zeros(shifts.shape, jnp.float32)
    for block in range(groups):
        matrix, weight, trans, p_start, p_end, g_ss, g_se, g_ee = pieces[block]
        inner = trans - coupling * starts[block][None, :] * matrix[NB - 1][:, None] - coupling * b_prev[None, :] * matrix[0][:, None]
        outputs.append(jnp.dot(matrix, weight * inner, precision=highest))
        b_prev = ends[block]
    return jnp.concatenate(outputs, axis=0)
```

```python
import functools

import jax
import jax.numpy as jnp
from jax import lax
from jax.experimental import pallas as pl
from jax.experimental.pallas import tpu as pltpu
from jax.sharding import PartitionSpec as P

coupling = 0.25
MESH = pl.DeviceIdType.MESH
LANES = 128
WIDE = 256


def split(value):
    high = value.astype(jnp.bfloat16)
    low = (value - high.astype(jnp.float32)).astype(jnp.bfloat16)
    return high, low


def product(stack, right_high, right_low):
    rows = stack.shape[0] // 2
    both = jnp.dot(stack[...], right_high, preferred_element_type=jnp.float32)
    last = jnp.dot(stack[:rows, :], right_low, preferred_element_type=jnp.float32)
    return both[:rows] + both[rows:] + last


def forward_state(q_prev, y_prev, coeffs):
    p_start, p_end, g_ss, g_se, g_ee = coeffs
    denom = 1.0 - coupling * g_ss * q_prev
    zero_part = (p_start - coupling * g_ss * y_prev) / denom
    one_part = p_end - coupling * g_se * y_prev + coupling * g_se * q_prev * zero_part
    q_zero = coupling * g_se / denom
    q_one = coupling * g_ee + coupling * g_se * q_prev * q_zero
    return (zero_part, one_part, q_zero, q_one)


def neighbour_values(parts, here, like):
    groups = len(parts)
    q_prev = y_prev = jnp.zeros_like(like)
    states = []
    for part in parts:
        state = forward_state(q_prev, y_prev, part)
        states.append(state)
        q_prev, y_prev = (state[3], state[1])
    a_next = jnp.zeros_like(like)
    mine_a = mine_b = jnp.zeros_like(like)
    for block in range(groups - 1, -1, -1):
        zero_part, one_part, q_zero, q_one = states[block]
        mine_a = jnp.where(here == block, a_next, mine_a)
        if block < groups - 1:
            mine_b = jnp.where(here == block + 1, one_part - q_one * a_next, mine_b)
        a_next = zero_part - q_zero * a_next
    return mine_a, mine_b


def send_all(count, axis, src, dst, send_sem, recv_sem):
    me = lax.axis_index(axis)
    copies = []
    for step in range(1, count):
        peer = lax.rem(me + step, count)
        copy = pltpu.make_async_remote_copy(
            src_ref=src,
            dst_ref=dst(me),
            send_sem=send_sem.at[step],
            recv_sem=recv_sem.at[step],
            device_id={axis: peer},
            device_id_type=MESH,
        )
        copy.start()
        copies.append(copy)
    return copies


def kernel(
    gathers, peers, groups,
    forcing, wavenumbers, eigvec, decay, out,
    f_buf, f_high, f_low, weight, trans, result, mine, matrix,
    stack, stack_t, rows_bc, g_mine, g_all, p_mine, p_all, edges,
    f_sem, v_send, v_recv, g_send, g_recv, p_send, p_recv, o_sem,
):
    points, lines = f_buf.shape
    chunks = lines // WIDE
    me = lax.axis_index("modes")
    here = lax.axis_index("gy")

    barrier = pltpu.get_barrier_semaphore()
    if gathers:
        for step in range(1, peers):
            pl.semaphore_signal(
                barrier, inc=1, device_id={"modes": lax.rem(me + step, peers)}, device_id_type=MESH
            )
    for step in range(1, groups):
        pl.semaphore_signal(
            barrier, inc=1, device_id={"gy": lax.rem(here + step, groups)}, device_id_type=MESH
        )
    loads = []
    for chunk in range(chunks):
        cols = pl.ds(chunk * WIDE, WIDE)
        load = pltpu.make_async_copy(forcing.at[:, cols], f_buf.at[:, cols], f_sem.at[chunk])
        load.start()
        loads.append(load)

    if gathers:
        rows = mine.shape[0]
        flat = eigvec[...]
        for row in range(rows):
            mine[row:row + 1, :] = flat[:, row * points:(row + 1) * points]
        pl.semaphore_wait(barrier, peers - 1 + groups - 1)
        sent = send_all(
            peers, "modes", mine,
            lambda at: matrix.at[pl.ds(pl.multiple_of(at * rows, 8), rows), :],
            v_send, v_recv,
        )
        matrix[pl.ds(pl.multiple_of(me * rows, 8), rows), :] = mine[...]
    else:
        pl.semaphore_wait(barrier, groups - 1)
        sent = []
        matrix[...] = eigvec[...]

    row_at = lax.broadcasted_iota(jnp.int32, (points, points), 0)
    col_at = lax.broadcasted_iota(jnp.int32, (points, points), 1)
    rate = jnp.sum(jnp.where(row_at == col_at, decay[...], 0.0), axis=1, keepdims=True)
    rate = jnp.broadcast_to(rate, (points, LANES))
    for chunk in range(lines // LANES):
        cols = slice(chunk * LANES, (chunk + 1) * LANES)
        kx = wavenumbers[0:1, cols].astype(jnp.float32) / 64.0
        kz = wavenumbers[1:2, cols].astype(jnp.float32) / 24.0
        weight[:, cols] = 1.0 / (kx * kx + kz * kz + rate)
    for chunk in range(chunks):
        cols = slice(chunk * WIDE, (chunk + 1) * WIDE)
        loads[chunk].wait()
        f_high[:, cols], f_low[:, cols] = split(f_buf[:, cols])

    for copy in sent:
        copy.wait()
    full = matrix[...]
    stack[:points, :], stack[points:, :] = split(full)
    turned = full.T
    stack_t[:points, :], stack_t[points:, :] = split(turned)
    first = jnp.broadcast_to(turned[:, 0:1], (points, LANES))
    last = jnp.broadcast_to(turned[:, points - 1:points], (points, LANES))
    rows_bc[0] = first
    rows_bc[1] = last
    rows_bc[2] = first * first
    rows_bc[3] = first * last
    rows_bc[4] = last * last

    for chunk in range(lines // LANES):
        part = weight[:, chunk * LANES:(chunk + 1) * LANES]
        for which in range(3):
            g_mine[which, chunk:chunk + 1, :] = jnp.sum(rows_bc[2 + which] * part, axis=0, keepdims=True)
    g_copies = send_all(groups, "gy", g_mine, lambda at: g_all.at[at], g_send, g_recv)
    g_all[here] = g_mine[...]

    for chunk in range(chunks):
        cols = slice(chunk * WIDE, (chunk + 1) * WIDE)
        value = product(stack_t, f_high[:, cols], f_low[:, cols])
        trans[:, cols] = value
        scaled = value * weight[:, cols]
        for half in range(WIDE // LANES):
            part = scaled[:, half * LANES:(half + 1) * LANES]
            row = chunk * (WIDE // LANES) + half
            for which in range(2):
                p_mine[which, row:row + 1, :] = jnp.sum(rows_bc[which] * part, axis=0, keepdims=True)
    p_copies = send_all(groups, "gy", p_mine, lambda at: p_all.at[at], p_send, p_recv)
    p_all[here] = p_mine[...]

    for copy in g_copies:
        copy.wait()
    for copy in p_copies:
        copy.wait()
    parts = [
        (p_all[block, 0], p_all[block, 1], g_all[block, 0], g_all[block, 1], g_all[block, 2])
        for block in range(groups)
    ]
    a_next, b_prev = neighbour_values(parts, here, parts[0][0])
    edges[0] = coupling * a_next
    edges[1] = coupling * b_prev

    stores = []
    for chunk in range(chunks):
        cols = slice(chunk * WIDE, (chunk + 1) * WIDE)
        halves = []
        for half in range(WIDE // LANES):
            row = chunk * (WIDE // LANES) + half
            lane = slice(row * LANES, (row + 1) * LANES)
            inner = (
                trans[:, lane]
                - edges[0, row:row + 1, :] * rows_bc[1]
                - edges[1, row:row + 1, :] * rows_bc[0]
            )
            halves.append(weight[:, lane] * inner)
        high, low = split(jnp.concatenate(halves, axis=1))
        result[:, cols] = product(stack, high, low)
        span = pl.ds(chunk * WIDE, WIDE)
        store = pltpu.make_async_copy(result.at[:, span], out.at[:, span], o_sem.at[chunk])
        store.start()
        stores.append(store)
    for store in stores:
        store.wait()


def local(peers, groups, forcing, wavenumbers, eigvec, decay):
    points, lines = forcing.shape
    held = eigvec.shape[1]
    gathers = held % (8 * points) == 0
    if not gathers:
        eigvec = lax.all_gather(eigvec, "modes", axis=1, tiled=True).reshape(points, points)
    rows = held // points if gathers else 8
    f32, bf16 = jnp.float32, jnp.bfloat16
    tall = lines // LANES
    chunks = lines // WIDE
    dma = pltpu.SemaphoreType.DMA
    vmem = pl.BlockSpec(memory_space=pltpu.VMEM)
    hbm = pl.BlockSpec(memory_space=pl.ANY)
    return pl.pallas_call(
        functools.partial(kernel, gathers, peers, groups),
        out_shape=jax.ShapeDtypeStruct((points, lines), f32),
        in_specs=[hbm, vmem, vmem, vmem],
        out_specs=hbm,
        scratch_shapes=[
            pltpu.VMEM((points, lines), f32),
            pltpu.VMEM((points, lines), bf16),
            pltpu.VMEM((points, lines), bf16),
            pltpu.VMEM((points, lines), f32),
            pltpu.VMEM((points, lines), f32),
            pltpu.VMEM((points, lines), f32),
            pltpu.VMEM((rows, points), f32),
            pltpu.VMEM((points, points), f32),
            pltpu.VMEM((2 * points, points), bf16),
            pltpu.VMEM((2 * points, points), bf16),
            pltpu.VMEM((5, points, LANES), f32),
            pltpu.VMEM((3, tall, LANES), f32),
            pltpu.VMEM((groups, 3, tall, LANES), f32),
            pltpu.VMEM((2, tall, LANES), f32),
            pltpu.VMEM((groups, 2, tall, LANES), f32),
            pltpu.VMEM((2, tall, LANES), f32),
            dma((chunks,)),
            dma((peers,)),
            dma((peers,)),
            dma((groups,)),
            dma((groups,)),
            dma((groups,)),
            dma((groups,)),
            dma((chunks,)),
        ],
        compiler_params=pltpu.CompilerParams(
            collective_id=0, has_side_effects=True, vmem_limit_bytes=32 * 1024 * 1024
        ),
        name="helmholtz",
    )(forcing, wavenumbers, eigvec, decay.reshape(1, points))


def solution(mesh):
    placed = (P("gy", "modes"), P(None, "modes"), P("gy", "modes"), P("gy"))
    return jax.shard_map(
        functools.partial(local, mesh.shape["modes"], mesh.shape["gy"]),
        mesh=mesh, in_specs=placed, out_specs=P("gy", "modes"), check_vma=False,
    )
```

```python
import functools

import jax
import jax.numpy as jnp
from jax import lax
from jax.experimental import pallas as pl
from jax.experimental.pallas import tpu as pltpu
from jax.sharding import PartitionSpec as P

coupling = 0.25
MESH = pl.DeviceIdType.MESH
LANES = 128
WIDE = 256


def split(value):
    high = value.astype(jnp.bfloat16)
    low = (value - high.astype(jnp.float32)).astype(jnp.bfloat16)
    return high, low


def product(stack, right_high, right_low):
    rows = stack.shape[0] // 2
    both = jnp.dot(stack[...], right_high, preferred_element_type=jnp.float32)
    last = jnp.dot(stack[:rows, :], right_low, preferred_element_type=jnp.float32)
    return both[:rows] + both[rows:] + last


def forward_state(q_prev, y_prev, coeffs):
    p_start, p_end, g_ss, g_se, g_ee = coeffs
    denom = 1.0 - coupling * g_ss * q_prev
    zero_part = (p_start - coupling * g_ss * y_prev) / denom
    one_part = p_end - coupling * g_se * y_prev + coupling * g_se * q_prev * zero_part
    q_zero = coupling * g_se / denom
    q_one = coupling * g_ee + coupling * g_se * q_prev * q_zero
    return (zero_part, one_part, q_zero, q_one)


def neighbour_values(parts, here, like):
    groups = len(parts)
    q_prev = y_prev = jnp.zeros_like(like)
    states = []
    for part in parts:
        state = forward_state(q_prev, y_prev, part)
        states.append(state)
        q_prev, y_prev = (state[3], state[1])
    a_next = jnp.zeros_like(like)
    mine_a = mine_b = jnp.zeros_like(like)
    for block in range(groups - 1, -1, -1):
        zero_part, one_part, q_zero, q_one = states[block]
        mine_a = jnp.where(here == block, a_next, mine_a)
        if block < groups - 1:
            mine_b = jnp.where(here == block + 1, one_part - q_one * a_next, mine_b)
        a_next = zero_part - q_zero * a_next
    return mine_a, mine_b


def send_all(count, axis, src, dst, send_sem, recv_sem):
    me = lax.axis_index(axis)
    copies = []
    for step in range(1, count):
        peer = lax.rem(me + step, count)
        copy = pltpu.make_async_remote_copy(
            src_ref=src,
            dst_ref=dst(me),
            send_sem=send_sem.at[step],
            recv_sem=recv_sem.at[step],
            device_id={axis: peer},
            device_id_type=MESH,
        )
        copy.start()
        copies.append(copy)
    return copies


def kernel(
    gathers, peers, groups,
    forcing, wavenumbers, eigvec, decay, out,
    eig, dec, numbers, f_buf, f_high, f_low, weight, trans, mine, matrix,
    stack, stack_t, rows_bc, g_mine, g_all, p_mine, p_all, edges,
    in_sem, f_sem, v_send, v_recv, g_send, g_recv, p_send, p_recv,
):
    points, lines = f_buf.shape
    chunks = lines // WIDE
    me = lax.axis_index("modes")
    here = lax.axis_index("gy")
    inner = 2 if peers % 2 == 0 else 1
    outer = peers // inner
    far, near = me // inner, lax.rem(me, inner)

    barrier = pltpu.get_barrier_semaphore()
    greeted = 0
    if gathers:
        for step in range(1, outer):
            peer = lax.rem(far + step, outer) * inner + near
            pl.semaphore_signal(barrier, inc=1, device_id={"modes": peer}, device_id_type=MESH)
        for step in range(1, inner):
            peer = far * inner + lax.rem(near + step, inner)
            pl.semaphore_signal(barrier, inc=1, device_id={"modes": peer}, device_id_type=MESH)
        greeted = outer + inner - 2
    for step in range(1, groups):
        pl.semaphore_signal(
            barrier, inc=1, device_id={"gy": lax.rem(here + step, groups)}, device_id_type=MESH
        )
    eig_load = pltpu.make_async_copy(eigvec, eig, in_sem.at[0])
    eig_load.start()
    dec_load = pltpu.make_async_copy(decay, dec, in_sem.at[1])
    dec_load.start()
    num_load = pltpu.make_async_copy(wavenumbers, numbers, in_sem.at[2])
    num_load.start()
    loads = []
    for chunk in range(chunks):
        cols = pl.ds(chunk * WIDE, WIDE)
        load = pltpu.make_async_copy(forcing.at[:, cols], f_buf.at[:, cols], f_sem.at[chunk])
        load.start()
        loads.append(load)

    eig_load.wait()
    rows = mine.shape[0]

    def slot(block):
        return matrix.at[pl.ds(pl.multiple_of(block * rows, 8), rows), :]

    def send(src, block, sems, peer):
        copy = pltpu.make_async_remote_copy(
            src_ref=src,
            dst_ref=slot(block),
            send_sem=v_send.at[sems],
            recv_sem=v_recv.at[sems],
            device_id={"modes": peer},
            device_id_type=MESH,
        )
        copy.start()
        return copy

    first_hop = []
    second_hop = []
    if gathers:
        flat = eig[...]
        for row in range(rows):
            mine[row:row + 1, :points] = flat[:, row * points:(row + 1) * points]
        pl.semaphore_wait(barrier, greeted + groups - 1)
        for step in range(1, outer):
            peer = lax.rem(far + step, outer) * inner + near
            first_hop.append(send(mine, me, step, peer))
        for step in range(1, inner):
            peer = far * inner + lax.rem(near + step, inner)
            second_hop.append(send(mine, me, step * outer, peer))
        matrix[pl.ds(pl.multiple_of(me * rows, 8), rows), :] = mine[...]
    else:
        pl.semaphore_wait(barrier, groups - 1)
        matrix[:, :points] = eig[...]

    dec_load.wait()
    num_load.wait()
    row_at = lax.broadcasted_iota(jnp.int32, (points, points), 0)
    col_at = lax.broadcasted_iota(jnp.int32, (points, points), 1)
    rate = jnp.sum(jnp.where(row_at == col_at, dec[...], 0.0), axis=1, keepdims=True)
    rate = jnp.broadcast_to(rate, (points, LANES))
    for chunk in range(lines // LANES):
        cols = slice(chunk * LANES, (chunk + 1) * LANES)
        kx = numbers[0:1, cols].astype(jnp.float32) / 64.0
        kz = numbers[1:2, cols].astype(jnp.float32) / 24.0
        weight[:, cols] = 1.0 / (kx * kx + kz * kz + rate)
    for step, copy in enumerate(first_hop, 1):
        copy.wait_recv()
        block = lax.rem(far + outer - step, outer) * inner + near
        for turn in range(1, inner):
            peer = far * inner + lax.rem(near + turn, inner)
            second_hop.append(send(slot(block), block, turn * outer + step, peer))
    for chunk in range(chunks):
        cols = slice(chunk * WIDE, (chunk + 1) * WIDE)
        loads[chunk].wait()
        f_high[:, cols], f_low[:, cols] = split(f_buf[:, cols])

    for copy in first_hop:
        copy.wait_send()
    for copy in second_hop:
        copy.wait()
    full = matrix[:, :points]
    stack[:points, :], stack[points:, :] = split(full)
    turned = full.T
    stack_t[:points, :], stack_t[points:, :] = split(turned)
    first = jnp.broadcast_to(turned[:, 0:1], (points, LANES))
    last = jnp.broadcast_to(turned[:, points - 1:points], (points, LANES))
    rows_bc[0] = first
    rows_bc[1] = last
    rows_bc[2] = first * first
    rows_bc[3] = first * last
    rows_bc[4] = last * last

    for chunk in range(lines // LANES):
        part = weight[:, chunk * LANES:(chunk + 1) * LANES]
        for which in range(3):
            g_mine[which, chunk:chunk + 1, :] = jnp.sum(rows_bc[2 + which] * part, axis=0, keepdims=True)
    g_copies = send_all(groups, "gy", g_mine, lambda at: g_all.at[at], g_send, g_recv)
    g_all[here] = g_mine[...]

    for chunk in range(chunks):
        cols = slice(chunk * WIDE, (chunk + 1) * WIDE)
        value = product(stack_t, f_high[:, cols], f_low[:, cols])
        trans[:, cols] = value
        scaled = value * weight[:, cols]
        for half in range(WIDE // LANES):
            part = scaled[:, half * LANES:(half + 1) * LANES]
            row = chunk * (WIDE // LANES) + half
            for which in range(2):
                p_mine[which, row:row + 1, :] = jnp.sum(rows_bc[which] * part, axis=0, keepdims=True)
    p_copies = send_all(groups, "gy", p_mine, lambda at: p_all.at[at], p_send, p_recv)
    p_all[here] = p_mine[...]

    for copy in g_copies:
        copy.wait()
    for copy in p_copies:
        copy.wait()
    parts = [
        (p_all[block, 0], p_all[block, 1], g_all[block, 0], g_all[block, 1], g_all[block, 2])
        for block in range(groups)
    ]
    a_next, b_prev = neighbour_values(parts, here, parts[0][0])
    edges[0] = coupling * a_next
    edges[1] = coupling * b_prev

    for chunk in range(chunks):
        cols = slice(chunk * WIDE, (chunk + 1) * WIDE)
        halves = []
        for half in range(WIDE // LANES):
            row = chunk * (WIDE // LANES) + half
            lane = slice(row * LANES, (row + 1) * LANES)
            bare = (
                trans[:, lane]
                - edges[0, row:row + 1, :] * rows_bc[1]
                - edges[1, row:row + 1, :] * rows_bc[0]
            )
            halves.append(weight[:, lane] * bare)
        high, low = split(jnp.concatenate(halves, axis=1))
        out[:, cols] = product(stack, high, low)


def local(peers, groups, forcing, wavenumbers, eigvec, decay):
    points, lines = forcing.shape
    held = eigvec.shape[1]
    gathers = held % (8 * points) == 0
    if not gathers:
        eigvec = lax.all_gather(eigvec, "modes", axis=1, tiled=True).reshape(points, points)
    rows = held // points if gathers else 8
    f32, bf16 = jnp.float32, jnp.bfloat16
    tall = lines // LANES
    padded = -(-points // LANES) * LANES
    chunks = lines // WIDE
    dma = pltpu.SemaphoreType.DMA
    vmem = pl.BlockSpec(memory_space=pltpu.VMEM)
    hbm = pl.BlockSpec(memory_space=pltpu.HBM)
    return pl.pallas_call(
        functools.partial(kernel, gathers, peers, groups),
        out_shape=jax.ShapeDtypeStruct((points, lines), f32),
        in_specs=[hbm, hbm, hbm, hbm],
        out_specs=vmem,
        scratch_shapes=[
            pltpu.VMEM(eigvec.shape, f32),
            pltpu.VMEM((1, points), f32),
            pltpu.VMEM(wavenumbers.shape, jnp.int32),
            pltpu.VMEM((points, lines), f32),
            pltpu.VMEM((points, lines), bf16),
            pltpu.VMEM((points, lines), bf16),
            pltpu.VMEM((points, lines), f32),
            pltpu.VMEM((points, lines), f32),
            pltpu.VMEM((rows, padded), f32),
            pltpu.VMEM((points, padded), f32),
            pltpu.VMEM((2 * points, points), bf16),
            pltpu.VMEM((2 * points, points), bf16),
            pltpu.VMEM((5, points, LANES), f32),
            pltpu.VMEM((3, tall, LANES), f32),
            pltpu.VMEM((groups, 3, tall, LANES), f32),
            pltpu.VMEM((2, tall, LANES), f32),
            pltpu.VMEM((groups, 2, tall, LANES), f32),
            pltpu.VMEM((2, tall, LANES), f32),
            dma((3,)),
            dma((chunks,)),
            dma((peers,)),
            dma((peers,)),
            dma((groups,)),
            dma((groups,)),
            dma((groups,)),
            dma((groups,)),
        ],
        compiler_params=pltpu.CompilerParams(
            collective_id=0, has_side_effects=True, vmem_limit_bytes=60 * 1024 * 1024
        ),
        name="helmholtz",
    )(forcing, wavenumbers, eigvec, decay.reshape(1, points))


def solution(mesh):
    placed = (P("gy", "modes"), P(None, "modes"), P("gy", "modes"), P("gy"))
    return jax.shard_map(
        functools.partial(local, mesh.shape["modes"], mesh.shape["gy"]),
        mesh=mesh, in_specs=placed, out_specs=P("gy", "modes"), check_vma=False,
    )
```

```python
import functools

import jax
import jax.numpy as jnp
from jax import lax
from jax.experimental import pallas as pl
from jax.experimental.pallas import tpu as pltpu
from jax.sharding import PartitionSpec as P

coupling = 0.25
MESH = pl.DeviceIdType.MESH
LANES = 128
WIDE = 256


def split(value):
    high = value.astype(jnp.bfloat16)
    low = (value - high.astype(jnp.float32)).astype(jnp.bfloat16)
    return high, low


def product(stack, right_high, right_low):
    rows = stack.shape[0] // 2
    both = jnp.dot(stack[...], right_high, preferred_element_type=jnp.float32)
    last = jnp.dot(stack[:rows, :], right_low, preferred_element_type=jnp.float32)
    return both[:rows] + both[rows:] + last


def forward_state(q_prev, y_prev, coeffs):
    p_start, p_end, g_ss, g_se, g_ee = coeffs
    denom = 1.0 - coupling * g_ss * q_prev
    zero_part = (p_start - coupling * g_ss * y_prev) / denom
    one_part = p_end - coupling * g_se * y_prev + coupling * g_se * q_prev * zero_part
    q_zero = coupling * g_se / denom
    q_one = coupling * g_ee + coupling * g_se * q_prev * q_zero
    return (zero_part, one_part, q_zero, q_one)


def neighbour_values(parts, here, like):
    groups = len(parts)
    q_prev = y_prev = jnp.zeros_like(like)
    states = []
    for part in parts:
        state = forward_state(q_prev, y_prev, part)
        states.append(state)
        q_prev, y_prev = (state[3], state[1])
    a_next = jnp.zeros_like(like)
    mine_a = mine_b = jnp.zeros_like(like)
    for block in range(groups - 1, -1, -1):
        zero_part, one_part, q_zero, q_one = states[block]
        mine_a = jnp.where(here == block, a_next, mine_a)
        if block < groups - 1:
            mine_b = jnp.where(here == block + 1, one_part - q_one * a_next, mine_b)
        a_next = zero_part - q_zero * a_next
    return mine_a, mine_b


def send_all(count, axis, src, dst, send_sem, recv_sem):
    me = lax.axis_index(axis)
    copies = []
    for step in range(1, count):
        peer = lax.rem(me + step, count)
        copy = pltpu.make_async_remote_copy(
            src_ref=src,
            dst_ref=dst(me),
            send_sem=send_sem.at[step],
            recv_sem=recv_sem.at[step],
            device_id={axis: peer},
            device_id_type=MESH,
        )
        copy.start()
        copies.append(copy)
    return copies


def kernel(
    gathers, peers, groups,
    forcing, wavenumbers, eigvec, decay, out,
    flat, dec, numbers, f_buf, f_high, f_low, weight, trans, mine, matrix,
    stack, stack_t, rows_bc, g_mine, g_all, p_mine, p_all, edges,
    in_sem, f_sem, v_send, v_recv, g_send, g_recv, p_send, p_recv,
):
    points, lines = f_buf.shape
    chunks = lines // WIDE
    me = lax.axis_index("modes")
    here = lax.axis_index("gy")
    inner = 2 if peers % 2 == 0 else 1
    outer = peers // inner
    far, near = me // inner, lax.rem(me, inner)

    barrier = pltpu.get_barrier_semaphore()
    greeted = 0
    if gathers:
        for step in range(1, outer):
            peer = lax.rem(far + step, outer) * inner + near
            pl.semaphore_signal(barrier, inc=1, device_id={"modes": peer}, device_id_type=MESH)
        for step in range(1, inner):
            peer = far * inner + lax.rem(near + step, inner)
            pl.semaphore_signal(barrier, inc=1, device_id={"modes": peer}, device_id_type=MESH)
        greeted = outer + inner - 2
    for step in range(1, groups):
        pl.semaphore_signal(
            barrier, inc=1, device_id={"gy": lax.rem(here + step, groups)}, device_id_type=MESH
        )
    eig_load = pltpu.make_async_copy(eigvec, flat.at[0] if gathers else flat, in_sem.at[0])
    eig_load.start()
    dec_load = pltpu.make_async_copy(decay, dec, in_sem.at[1])
    dec_load.start()
    num_load = pltpu.make_async_copy(wavenumbers, numbers, in_sem.at[2])
    num_load.start()
    loads = []
    for chunk in range(chunks):
        cols = pl.ds(chunk * WIDE, WIDE)
        load = pltpu.make_async_copy(forcing.at[:, cols], f_buf.at[:, cols], f_sem.at[chunk])
        load.start()
        loads.append(load)

    rows = mine.shape[1]

    def send(src, place, peer):
        copy = pltpu.make_async_remote_copy(
            src_ref=src,
            dst_ref=flat.at[place],
            send_sem=v_send.at[place],
            recv_sem=v_recv.at[place],
            device_id={"modes": peer},
            device_id_type=MESH,
        )
        copy.start()
        return copy

    def unpack(place, block):
        line = flat[place]
        for row in range(rows):
            mine[place, row:row + 1, :points] = line[:, row * points:(row + 1) * points]
        matrix[pl.ds(pl.multiple_of(block * rows, 8), rows), :] = mine[place]

    def near_peer(turn):
        return far * inner + lax.rem(near + turn, inner)

    hops = {}
    if gathers:
        pl.semaphore_wait(barrier, greeted + groups - 1)
        for step in range(1, outer):
            hops[step] = send(eigvec, step, lax.rem(far + step, outer) * inner + near)
        for turn in range(1, inner):
            hops[turn * outer] = send(eigvec, turn * outer, near_peer(turn))
        eig_load.wait()
        unpack(0, me)
    else:
        pl.semaphore_wait(barrier, groups - 1)
        eig_load.wait()
        matrix[:, :points] = flat[...]

    dec_load.wait()
    num_load.wait()
    row_at = lax.broadcasted_iota(jnp.int32, (points, points), 0)
    col_at = lax.broadcasted_iota(jnp.int32, (points, points), 1)
    rate = jnp.sum(jnp.where(row_at == col_at, dec[...], 0.0), axis=1, keepdims=True)
    rate = jnp.broadcast_to(rate, (points, LANES))
    for chunk in range(lines // LANES):
        cols = slice(chunk * LANES, (chunk + 1) * LANES)
        kx = numbers[0:1, cols].astype(jnp.float32) / 64.0
        kz = numbers[1:2, cols].astype(jnp.float32) / 24.0
        weight[:, cols] = 1.0 / (kx * kx + kz * kz + rate)
    if gathers:
        for step in range(1, outer):
            hops[step].wait_recv()
            for turn in range(1, inner):
                place = turn * outer + step
                hops[place] = send(flat.at[step], place, near_peer(turn))
        for step in range(1, outer):
            unpack(step, lax.rem(far + outer - step, outer) * inner + near)
    for chunk in range(chunks):
        cols = slice(chunk * WIDE, (chunk + 1) * WIDE)
        loads[chunk].wait()
        f_high[:, cols], f_low[:, cols] = split(f_buf[:, cols])
    if gathers:
        for turn in range(1, inner):
            for step in range(outer):
                place = turn * outer + step
                hops[place].wait_recv()
                unpack(
                    place,
                    lax.rem(far + outer - step, outer) * inner + lax.rem(near + inner - turn, inner),
                )
        for copy in hops.values():
            copy.wait_send()
    full = matrix[:, :points]
    stack[:points, :], stack[points:, :] = split(full)
    turned = full.T
    stack_t[:points, :], stack_t[points:, :] = split(turned)
    first = jnp.broadcast_to(turned[:, 0:1], (points, LANES))
    last = jnp.broadcast_to(turned[:, points - 1:points], (points, LANES))
    rows_bc[0] = first
    rows_bc[1] = last
    rows_bc[2] = first * first
    rows_bc[3] = first * last
    rows_bc[4] = last * last

    per = WIDE // LANES
    g_copies = []
    for chunk in range(chunks):
        cols = slice(chunk * WIDE, (chunk + 1) * WIDE)
        if 2 * chunk < chunks:
            for row in range(2 * chunk * per, min(2 * chunk + 2, chunks) * per):
                part = weight[:, row * LANES:(row + 1) * LANES]
                for which in range(3):
                    g_mine[which, row:row + 1, :] = jnp.sum(
                        rows_bc[2 + which] * part, axis=0, keepdims=True
                    )
            if 2 * chunk + 2 >= chunks:
                g_copies = send_all(groups, "gy", g_mine, lambda at: g_all.at[at], g_send, g_recv)
                g_all[here] = g_mine[...]
        value = product(stack_t, f_high[:, cols], f_low[:, cols])
        trans[:, cols] = value
        scaled = value * weight[:, cols]
        for half in range(WIDE // LANES):
            part = scaled[:, half * LANES:(half + 1) * LANES]
            row = chunk * (WIDE // LANES) + half
            for which in range(2):
                p_mine[which, row:row + 1, :] = jnp.sum(rows_bc[which] * part, axis=0, keepdims=True)
    p_copies = send_all(groups, "gy", p_mine, lambda at: p_all.at[at], p_send, p_recv)
    p_all[here] = p_mine[...]

    for copy in g_copies:
        copy.wait()
    for copy in p_copies:
        copy.wait()
    parts = [
        (p_all[block, 0], p_all[block, 1], g_all[block, 0], g_all[block, 1], g_all[block, 2])
        for block in range(groups)
    ]
    a_next, b_prev = neighbour_values(parts, here, parts[0][0])
    edges[0] = coupling * a_next
    edges[1] = coupling * b_prev

    for chunk in range(chunks):
        cols = slice(chunk * WIDE, (chunk + 1) * WIDE)
        halves = []
        for half in range(WIDE // LANES):
            row = chunk * (WIDE // LANES) + half
            lane = slice(row * LANES, (row + 1) * LANES)
            bare = (
                trans[:, lane]
                - edges[0, row:row + 1, :] * rows_bc[1]
                - edges[1, row:row + 1, :] * rows_bc[0]
            )
            halves.append(weight[:, lane] * bare)
        high, low = split(jnp.concatenate(halves, axis=1))
        out[:, cols] = product(stack, high, low)


def local(peers, groups, forcing, wavenumbers, eigvec, decay):
    points, lines = forcing.shape
    held = eigvec.shape[1]
    gathers = held % (8 * points) == 0
    if not gathers:
        eigvec = lax.all_gather(eigvec, "modes", axis=1, tiled=True).reshape(points, points)
    rows = held // points if gathers else 8
    f32, bf16 = jnp.float32, jnp.bfloat16
    tall = lines // LANES
    padded = -(-points // LANES) * LANES
    chunks = lines // WIDE
    dma = pltpu.SemaphoreType.DMA
    vmem = pl.BlockSpec(memory_space=pltpu.VMEM)
    hbm = pl.BlockSpec(memory_space=pltpu.HBM)
    return pl.pallas_call(
        functools.partial(kernel, gathers, peers, groups),
        out_shape=jax.ShapeDtypeStruct((points, lines), f32),
        in_specs=[hbm, hbm, hbm, hbm],
        out_specs=vmem,
        scratch_shapes=[
            pltpu.VMEM((peers, *eigvec.shape) if gathers else eigvec.shape, f32),
            pltpu.VMEM((1, points), f32),
            pltpu.VMEM(wavenumbers.shape, jnp.int32),
            pltpu.VMEM((points, lines), f32),
            pltpu.VMEM((points, lines), bf16),
            pltpu.VMEM((points, lines), bf16),
            pltpu.VMEM((points, lines), f32),
            pltpu.VMEM((points, lines), f32),
            pltpu.VMEM((peers if gathers else 1, rows, padded), f32),
            pltpu.VMEM((points, padded), f32),
            pltpu.VMEM((2 * points, points), bf16),
            pltpu.VMEM((2 * points, points), bf16),
            pltpu.VMEM((5, points, LANES), f32),
            pltpu.VMEM((3, tall, LANES), f32),
            pltpu.VMEM((groups, 3, tall, LANES), f32),
            pltpu.VMEM((2, tall, LANES), f32),
            pltpu.VMEM((groups, 2, tall, LANES), f32),
            pltpu.VMEM((2, tall, LANES), f32),
            dma((3,)),
            dma((chunks,)),
            dma((peers,)),
            dma((peers,)),
            dma((groups,)),
            dma((groups,)),
            dma((groups,)),
            dma((groups,)),
        ],
        compiler_params=pltpu.CompilerParams(
            collective_id=0, has_side_effects=True, vmem_limit_bytes=32 * 1024 * 1024
        ),
        name="helmholtz",
    )(*[
        pltpu.with_memory_space_constraint(operand, pltpu.HBM)
        for operand in (forcing, wavenumbers, eigvec, decay.reshape(1, points))
    ])


def solution(mesh):
    placed = (P("gy", "modes"), P(None, "modes"), P("gy", "modes"), P("gy"))
    return jax.shard_map(
        functools.partial(local, mesh.shape["modes"], mesh.shape["gy"]),
        mesh=mesh, in_specs=placed, out_specs=P("gy", "modes"), check_vma=False,
    )
```

```python
import functools

import jax
import jax.numpy as jnp
from jax import lax
from jax.experimental import pallas as pl
from jax.experimental.pallas import tpu as pltpu
from jax.sharding import PartitionSpec as P

coupling = 0.25
MESH = pl.DeviceIdType.MESH
LANES = 128
WIDE = 256


def split(value):
    high = value.astype(jnp.bfloat16)
    low = (value - high.astype(jnp.float32)).astype(jnp.bfloat16)
    return high, low


def product(stack, right_high, right_low):
    rows = stack.shape[0] // 2
    both = jnp.dot(stack[...], right_high, preferred_element_type=jnp.float32)
    last = jnp.dot(stack[:rows, :], right_low, preferred_element_type=jnp.float32)
    return both[:rows] + both[rows:] + last


def forward_state(q_prev, y_prev, coeffs):
    p_start, p_end, g_ss, g_se, g_ee = coeffs
    denom = 1.0 - coupling * g_ss * q_prev
    zero_part = (p_start - coupling * g_ss * y_prev) / denom
    one_part = p_end - coupling * g_se * y_prev + coupling * g_se * q_prev * zero_part
    q_zero = coupling * g_se / denom
    q_one = coupling * g_ee + coupling * g_se * q_prev * q_zero
    return (zero_part, one_part, q_zero, q_one)


def neighbour_values(parts, here, like):
    groups = len(parts)
    q_prev = y_prev = jnp.zeros_like(like)
    states = []
    for part in parts:
        state = forward_state(q_prev, y_prev, part)
        states.append(state)
        q_prev, y_prev = (state[3], state[1])
    a_next = jnp.zeros_like(like)
    mine_a = mine_b = jnp.zeros_like(like)
    for block in range(groups - 1, -1, -1):
        zero_part, one_part, q_zero, q_one = states[block]
        mine_a = jnp.where(here == block, a_next, mine_a)
        if block < groups - 1:
            mine_b = jnp.where(here == block + 1, one_part - q_one * a_next, mine_b)
        a_next = zero_part - q_zero * a_next
    return mine_a, mine_b


def send_all(count, axis, src, dst, send_sem, recv_sem):
    me = lax.axis_index(axis)
    copies = []
    for step in range(1, count):
        peer = lax.rem(me + step, count)
        copy = pltpu.make_async_remote_copy(
            src_ref=src,
            dst_ref=dst(me),
            send_sem=send_sem.at[step],
            recv_sem=recv_sem.at[step],
            device_id={axis: peer},
            device_id_type=MESH,
        )
        copy.start()
        copies.append(copy)
    return copies


def inverse(value):
    near = pl.reciprocal(value, approx=True)
    return near * (2.0 - value * near)


def kernel(
    gathers, peers, groups,
    forcing, wavenumbers, eigvec, decay,
    weight, trans, stack, rows_bc, edges,
    flat, dec, numbers, f_buf, f_high, f_low, mine, matrix,
    stack_t, g_mine, g_all, p_mine, p_all,
    in_sem, f_sem, v_send, v_recv, g_send, g_recv, p_send, p_recv,
):
    points, lines = f_buf.shape
    chunks = lines // WIDE
    me = lax.axis_index("modes")
    here = lax.axis_index("gy")
    inner = 2 if peers % 2 == 0 else 1
    outer = peers // inner
    far, near = me // inner, lax.rem(me, inner)

    barrier = pltpu.get_barrier_semaphore()
    greeted = 0
    if gathers:
        for step in range(1, outer):
            peer = lax.rem(far + step, outer) * inner + near
            pl.semaphore_signal(barrier, inc=1, device_id={"modes": peer}, device_id_type=MESH)
        for step in range(1, inner):
            peer = far * inner + lax.rem(near + step, inner)
            pl.semaphore_signal(barrier, inc=1, device_id={"modes": peer}, device_id_type=MESH)
        greeted = outer + inner - 2
    for step in range(1, groups):
        pl.semaphore_signal(
            barrier, inc=1, device_id={"gy": lax.rem(here + step, groups)}, device_id_type=MESH
        )
    eig_load = pltpu.make_async_copy(eigvec, flat.at[0] if gathers else flat, in_sem.at[0])
    eig_load.start()
    dec_load = pltpu.make_async_copy(decay, dec, in_sem.at[1])
    dec_load.start()
    num_load = pltpu.make_async_copy(wavenumbers, numbers, in_sem.at[2])
    num_load.start()
    loads = []
    for chunk in range(chunks):
        cols = pl.ds(chunk * WIDE, WIDE)
        load = pltpu.make_async_copy(forcing.at[:, cols], f_buf.at[:, cols], f_sem.at[chunk])
        load.start()
        loads.append(load)

    rows = mine.shape[1]

    def send(src, place, peer):
        copy = pltpu.make_async_remote_copy(
            src_ref=src,
            dst_ref=flat.at[place],
            send_sem=v_send.at[place],
            recv_sem=v_recv.at[place],
            device_id={"modes": peer},
            device_id_type=MESH,
        )
        copy.start()
        return copy

    def unpack(place, block):
        line = flat[place]
        for row in range(rows):
            mine[place, row:row + 1, :points] = line[:, row * points:(row + 1) * points]
        matrix[pl.ds(pl.multiple_of(block * rows, 8), rows), :] = mine[place]

    def near_peer(turn):
        return far * inner + lax.rem(near + turn, inner)

    hops = {}
    if gathers:
        pl.semaphore_wait(barrier, greeted + groups - 1)
        for step in range(1, outer):
            hops[step] = send(eigvec, step, lax.rem(far + step, outer) * inner + near)
        for turn in range(1, inner):
            hops[turn * outer] = send(eigvec, turn * outer, near_peer(turn))
        eig_load.wait()
        unpack(0, me)
    else:
        pl.semaphore_wait(barrier, groups - 1)
        eig_load.wait()
        matrix[:, :points] = flat[...]

    dec_load.wait()
    num_load.wait()
    row_at = lax.broadcasted_iota(jnp.int32, (points, points), 0)
    col_at = lax.broadcasted_iota(jnp.int32, (points, points), 1)
    rate = jnp.sum(jnp.where(row_at == col_at, dec[...], 0.0), axis=1, keepdims=True)
    rate = jnp.broadcast_to(rate, (points, LANES))
    for chunk in range(lines // LANES):
        cols = slice(chunk * LANES, (chunk + 1) * LANES)
        kx = numbers[0:1, cols].astype(jnp.float32) / 64.0
        kz = numbers[1:2, cols].astype(jnp.float32) / 24.0
        weight[:, cols] = inverse(kx * kx + kz * kz + rate)
    if gathers:
        for step in range(1, outer):
            hops[step].wait_recv()
            for turn in range(1, inner):
                place = turn * outer + step
                hops[place] = send(flat.at[step], place, near_peer(turn))
        for step in range(1, outer):
            unpack(step, lax.rem(far + outer - step, outer) * inner + near)
    for chunk in range(chunks):
        cols = slice(chunk * WIDE, (chunk + 1) * WIDE)
        loads[chunk].wait()
        f_high[:, cols], f_low[:, cols] = split(f_buf[:, cols])
    if gathers:
        for turn in range(1, inner):
            for step in range(outer):
                place = turn * outer + step
                hops[place].wait_recv()
                unpack(
                    place,
                    lax.rem(far + outer - step, outer) * inner + lax.rem(near + inner - turn, inner),
                )
        for copy in hops.values():
            copy.wait_send()
    full = matrix[:, :points]
    stack[:points, :], stack[points:, :] = split(full)
    turned = full.T
    stack_t[:points, :], stack_t[points:, :] = split(turned)
    first = jnp.broadcast_to(turned[:, 0:1], (points, LANES))
    last = jnp.broadcast_to(turned[:, points - 1:points], (points, LANES))
    rows_bc[0] = first
    rows_bc[1] = last
    rows_bc[2] = first * first
    rows_bc[3] = first * last
    rows_bc[4] = last * last

    per = WIDE // LANES
    g_copies = []
    for chunk in range(chunks):
        cols = slice(chunk * WIDE, (chunk + 1) * WIDE)
        if 2 * chunk < chunks:
            for row in range(2 * chunk * per, min(2 * chunk + 2, chunks) * per):
                part = weight[:, row * LANES:(row + 1) * LANES]
                for which in range(3):
                    g_mine[which, row:row + 1, :] = jnp.sum(
                        rows_bc[2 + which] * part, axis=0, keepdims=True
                    )
            if 2 * chunk + 2 >= chunks:
                g_copies = send_all(groups, "gy", g_mine, lambda at: g_all.at[at], g_send, g_recv)
                g_all[here] = g_mine[...]
        value = product(stack_t, f_high[:, cols], f_low[:, cols])
        trans[:, cols] = value
        scaled = value * weight[:, cols]
        for half in range(WIDE // LANES):
            part = scaled[:, half * LANES:(half + 1) * LANES]
            row = chunk * (WIDE // LANES) + half
            for which in range(2):
                p_mine[which, row:row + 1, :] = jnp.sum(rows_bc[which] * part, axis=0, keepdims=True)
    p_copies = send_all(groups, "gy", p_mine, lambda at: p_all.at[at], p_send, p_recv)
    p_all[here] = p_mine[...]

    for copy in g_copies:
        copy.wait()
    for copy in p_copies:
        copy.wait()
    parts = [
        (p_all[block, 0], p_all[block, 1], g_all[block, 0], g_all[block, 1], g_all[block, 2])
        for block in range(groups)
    ]
    a_next, b_prev = neighbour_values(parts, here, parts[0][0])
    edges[0] = coupling * a_next
    edges[1] = coupling * b_prev


def finish(weight, trans, stack, rows_bc, edges, out, result, sem):
    points, lines = trans.shape
    stores = []
    for chunk in range(lines // WIDE):
        halves = []
        for half in range(WIDE // LANES):
            row = chunk * (WIDE // LANES) + half
            lane = slice(row * LANES, (row + 1) * LANES)
            bare = (
                trans[:, lane]
                - edges[0, row:row + 1, :] * rows_bc[1]
                - edges[1, row:row + 1, :] * rows_bc[0]
            )
            halves.append(weight[:, lane] * bare)
        high, low = split(jnp.concatenate(halves, axis=1))
        span = pl.ds(chunk * WIDE, WIDE)
        result[:, span] = product(stack, high, low)
        store = pltpu.make_async_copy(result.at[:, span], out.at[:, span], sem.at[chunk])
        store.start()
        stores.append(store)
    for store in stores:
        store.wait()


def local(peers, groups, forcing, wavenumbers, eigvec, decay):
    points, lines = forcing.shape
    held = eigvec.shape[1]
    gathers = held % (8 * points) == 0
    if not gathers:
        eigvec = lax.all_gather(eigvec, "modes", axis=1, tiled=True).reshape(points, points)
    rows = held // points if gathers else 8
    f32, bf16 = jnp.float32, jnp.bfloat16
    tall = lines // LANES
    padded = -(-points // LANES) * LANES
    chunks = lines // WIDE
    dma = pltpu.SemaphoreType.DMA
    vmem = pl.BlockSpec(memory_space=pltpu.VMEM)
    hbm = pl.BlockSpec(memory_space=pltpu.HBM)
    solved = pl.pallas_call(
        functools.partial(kernel, gathers, peers, groups),
        out_shape=(
            jax.ShapeDtypeStruct((points, lines), f32),
            jax.ShapeDtypeStruct((points, lines), f32),
            jax.ShapeDtypeStruct((2 * points, points), bf16),
            jax.ShapeDtypeStruct((5, points, LANES), f32),
            jax.ShapeDtypeStruct((2, tall, LANES), f32),
        ),
        in_specs=[hbm, hbm, hbm, hbm],
        out_specs=(vmem,) * 5,
        scratch_shapes=[
            pltpu.VMEM((peers, *eigvec.shape) if gathers else eigvec.shape, f32),
            pltpu.VMEM((1, points), f32),
            pltpu.VMEM(wavenumbers.shape, jnp.int32),
            pltpu.VMEM((points, lines), f32),
            pltpu.VMEM((points, lines), bf16),
            pltpu.VMEM((points, lines), bf16),
            pltpu.VMEM((peers if gathers else 1, rows, padded), f32),
            pltpu.VMEM((points, padded), f32),
            pltpu.VMEM((2 * points, points), bf16),
            pltpu.VMEM((3, tall, LANES), f32),
            pltpu.VMEM((groups, 3, tall, LANES), f32),
            pltpu.VMEM((2, tall, LANES), f32),
            pltpu.VMEM((groups, 2, tall, LANES), f32),
            dma((3,)),
            dma((chunks,)),
            dma((peers,)),
            dma((peers,)),
            dma((groups,)),
            dma((groups,)),
            dma((groups,)),
            dma((groups,)),
        ],
        compiler_params=pltpu.CompilerParams(
            collective_id=0, has_side_effects=True, vmem_limit_bytes=32 * 1024 * 1024
        ),
        name="helmholtz",
    )(*[
        pltpu.with_memory_space_constraint(operand, pltpu.HBM)
        for operand in (forcing, wavenumbers, eigvec, decay.reshape(1, points))
    ])
    return pl.pallas_call(
        finish,
        out_shape=jax.ShapeDtypeStruct((points, lines), f32),
        in_specs=[vmem] * 5,
        out_specs=hbm,
        scratch_shapes=[pltpu.VMEM((points, lines), f32), dma((chunks,))],
        compiler_params=pltpu.CompilerParams(vmem_limit_bytes=16 * 1024 * 1024),
        name="finish",
    )(*solved)


def solution(mesh):
    placed = (P("gy", "modes"), P(None, "modes"), P("gy", "modes"), P("gy"))
    return jax.shard_map(
        functools.partial(local, mesh.shape["modes"], mesh.shape["gy"]),
        mesh=mesh, in_specs=placed, out_specs=P("gy", "modes"), check_vma=False,
    )
```

```python
import functools

import jax
import jax.numpy as jnp
from jax import lax
from jax.experimental import pallas as pl
from jax.experimental.pallas import tpu as pltpu
from jax.sharding import PartitionSpec as P

coupling = 0.25
MESH = pl.DeviceIdType.MESH
LANES = 128
WIDE = 256


def split(value):
    high = value.astype(jnp.bfloat16)
    low = (value - high.astype(jnp.float32)).astype(jnp.bfloat16)
    return high, low


def product(stack, right_high, right_low):
    rows = stack.shape[0] // 2
    both = jnp.dot(stack[...], right_high, preferred_element_type=jnp.float32)
    last = jnp.dot(stack[:rows, :], right_low, preferred_element_type=jnp.float32)
    return both[:rows] + both[rows:] + last


def corner_states(corners):
    q_prev = jnp.zeros_like(corners[0][0])
    states = []
    for g_ss, g_se, g_ee in corners:
        scale = 1.0 / (1.0 - coupling * g_ss * q_prev)
        q_zero = coupling * g_se * scale
        q_one = coupling * g_ee + coupling * g_se * q_prev * q_zero
        states.append((scale, coupling * g_ss, coupling * g_se, coupling * g_se * q_prev, q_zero, q_one))
        q_prev = q_one
    return states


def neighbour_values(states, edge_values, here):
    groups = len(states)
    zero = jnp.zeros_like(edge_values[0][0])
    y_prev = zero
    values = []
    for (p_start, p_end), (scale, c_ss, c_se, c_seq, _, _) in zip(edge_values, states):
        zero_part = (p_start - c_ss * y_prev) * scale
        one_part = p_end - c_se * y_prev + c_seq * zero_part
        values.append((zero_part, one_part))
        y_prev = one_part
    a_next = mine_a = mine_b = zero
    for block in range(groups - 1, -1, -1):
        zero_part, one_part = values[block]
        q_zero, q_one = states[block][4:]
        mine_a = jnp.where(here == block, a_next, mine_a)
        if block < groups - 1:
            mine_b = jnp.where(here == block + 1, one_part - q_one * a_next, mine_b)
        a_next = zero_part - q_zero * a_next
    return mine_a, mine_b


def send_all(count, axis, src, dst, send_sem, recv_sem):
    me = lax.axis_index(axis)
    copies = []
    for step in range(1, count):
        peer = lax.rem(me + step, count)
        copy = pltpu.make_async_remote_copy(
            src_ref=src,
            dst_ref=dst(me),
            send_sem=send_sem.at[step],
            recv_sem=recv_sem.at[step],
            device_id={axis: peer},
            device_id_type=MESH,
        )
        copy.start()
        copies.append(copy)
    return copies


def inverse(value):
    near = pl.reciprocal(value, approx=True)
    return near * (2.0 - value * near)


def kernel(
    gathers, peers, groups,
    forcing, wavenumbers, eigvec, decay,
    weight, trans, stack, rows_bc, edges,
    flat, dec, numbers, f_buf, f_high, f_low, mine, matrix,
    stack_t, g_mine, g_all, p_mine, p_all,
    in_sem, f_sem, v_send, v_recv, g_send, g_recv, p_send, p_recv,
):
    points, lines = f_buf.shape
    chunks = lines // WIDE
    me = lax.axis_index("modes")
    here = lax.axis_index("gy")

    barrier = pltpu.get_barrier_semaphore()
    greeted = 0
    if gathers:
        for step in range(1, peers):
            pl.semaphore_signal(
                barrier, inc=1, device_id={"modes": lax.rem(me + step, peers)}, device_id_type=MESH
            )
        greeted = peers - 1
    for step in range(1, groups):
        pl.semaphore_signal(
            barrier, inc=1, device_id={"gy": lax.rem(here + step, groups)}, device_id_type=MESH
        )
    eig_load = pltpu.make_async_copy(eigvec, flat.at[0] if gathers else flat, in_sem.at[0])
    eig_load.start()
    dec_load = pltpu.make_async_copy(decay, dec, in_sem.at[1])
    dec_load.start()
    num_load = pltpu.make_async_copy(wavenumbers, numbers, in_sem.at[2])
    num_load.start()
    loads = []
    for chunk in range(chunks):
        cols = pl.ds(chunk * WIDE, WIDE)
        load = pltpu.make_async_copy(forcing.at[:, cols], f_buf.at[:, cols], f_sem.at[chunk])
        load.start()
        loads.append(load)

    rows = mine.shape[1]

    def unpack(place, block):
        line = flat[place]
        for row in range(rows):
            mine[place, row:row + 1, :points] = line[:, row * points:(row + 1) * points]
        matrix[pl.ds(pl.multiple_of(block * rows, 8), rows), :] = mine[place]

    hops = []
    if gathers:
        eig_load.wait()
        pl.semaphore_wait(barrier, greeted + groups - 1)
        for step in range(1, peers):
            copy = pltpu.make_async_remote_copy(
                src_ref=flat.at[0],
                dst_ref=flat.at[step],
                send_sem=v_send.at[step],
                recv_sem=v_recv.at[step],
                device_id={"modes": lax.rem(me + step, peers)},
                device_id_type=MESH,
            )
            copy.start()
            hops.append(copy)
        unpack(0, me)
    else:
        pl.semaphore_wait(barrier, groups - 1)
        eig_load.wait()
        matrix[:, :points] = flat[...]

    dec_load.wait()
    num_load.wait()
    row_at = lax.broadcasted_iota(jnp.int32, (points, points), 0)
    col_at = lax.broadcasted_iota(jnp.int32, (points, points), 1)
    rate = jnp.sum(jnp.where(row_at == col_at, dec[...], 0.0), axis=1, keepdims=True)
    rate = jnp.broadcast_to(rate, (points, LANES))
    for chunk in range(lines // LANES):
        cols = slice(chunk * LANES, (chunk + 1) * LANES)
        kx = numbers[0:1, cols].astype(jnp.float32) / 64.0
        kz = numbers[1:2, cols].astype(jnp.float32) / 24.0
        weight[:, cols] = inverse(kx * kx + kz * kz + rate)
    for chunk in range(chunks):
        cols = slice(chunk * WIDE, (chunk + 1) * WIDE)
        loads[chunk].wait()
        f_high[:, cols], f_low[:, cols] = split(f_buf[:, cols])
    for step, copy in enumerate(hops, 1):
        copy.wait_recv()
        unpack(step, lax.rem(me + peers - step, peers))
    for copy in hops:
        copy.wait_send()
    full = matrix[:, :points]
    stack[:points, :], stack[points:, :] = split(full)
    turned = full.T
    stack_t[:points, :], stack_t[points:, :] = split(turned)
    first = jnp.broadcast_to(turned[:, 0:1], (points, LANES))
    last = jnp.broadcast_to(turned[:, points - 1:points], (points, LANES))
    rows_bc[0] = first
    rows_bc[1] = last
    rows_bc[2] = first * first
    rows_bc[3] = first * last
    rows_bc[4] = last * last

    per = WIDE // LANES
    g_copies = []
    for chunk in range(chunks):
        cols = slice(chunk * WIDE, (chunk + 1) * WIDE)
        if 2 * chunk < chunks:
            for row in range(2 * chunk * per, min(2 * chunk + 2, chunks) * per):
                part = weight[:, row * LANES:(row + 1) * LANES]
                for which in range(3):
                    g_mine[which, row:row + 1, :] = jnp.sum(
                        rows_bc[2 + which] * part, axis=0, keepdims=True
                    )
            if 2 * chunk + 2 >= chunks:
                g_copies = send_all(groups, "gy", g_mine, lambda at: g_all.at[at], g_send, g_recv)
                g_all[here] = g_mine[...]
        value = product(stack_t, f_high[:, cols], f_low[:, cols])
        trans[:, cols] = value
        scaled = value * weight[:, cols]
        for half in range(WIDE // LANES):
            part = scaled[:, half * LANES:(half + 1) * LANES]
            row = chunk * (WIDE // LANES) + half
            for which in range(2):
                p_mine[which, row:row + 1, :] = jnp.sum(rows_bc[which] * part, axis=0, keepdims=True)
    p_copies = send_all(groups, "gy", p_mine, lambda at: p_all.at[at], p_send, p_recv)
    p_all[here] = p_mine[...]

    for copy in g_copies:
        copy.wait()
    states = corner_states(
        [(g_all[block, 0], g_all[block, 1], g_all[block, 2]) for block in range(groups)]
    )
    for copy in p_copies:
        copy.wait()
    a_next, b_prev = neighbour_values(
        states, [(p_all[block, 0], p_all[block, 1]) for block in range(groups)], here
    )
    edges[0] = coupling * a_next
    edges[1] = coupling * b_prev


def finish(weight, trans, stack, rows_bc, edges, out, result, sem):
    points, lines = trans.shape
    stores = []
    for chunk in range(lines // WIDE):
        halves = []
        for half in range(WIDE // LANES):
            row = chunk * (WIDE // LANES) + half
            lane = slice(row * LANES, (row + 1) * LANES)
            bare = (
                trans[:, lane]
                - edges[0, row:row + 1, :] * rows_bc[1]
                - edges[1, row:row + 1, :] * rows_bc[0]
            )
            halves.append(weight[:, lane] * bare)
        high, low = split(jnp.concatenate(halves, axis=1))
        span = pl.ds(chunk * WIDE, WIDE)
        result[:, span] = product(stack, high, low)
        store = pltpu.make_async_copy(result.at[:, span], out.at[:, span], sem.at[chunk])
        store.start()
        stores.append(store)
    for store in stores:
        store.wait()


def local(peers, groups, forcing, wavenumbers, eigvec, decay):
    points, lines = forcing.shape
    held = eigvec.shape[1]
    gathers = held % (8 * points) == 0
    if not gathers:
        eigvec = lax.all_gather(eigvec, "modes", axis=1, tiled=True).reshape(points, points)
    rows = held // points if gathers else 8
    f32, bf16 = jnp.float32, jnp.bfloat16
    tall = lines // LANES
    padded = -(-points // LANES) * LANES
    chunks = lines // WIDE
    dma = pltpu.SemaphoreType.DMA
    vmem = pl.BlockSpec(memory_space=pltpu.VMEM)
    hbm = pl.BlockSpec(memory_space=pltpu.HBM)
    solved = pl.pallas_call(
        functools.partial(kernel, gathers, peers, groups),
        out_shape=(
            jax.ShapeDtypeStruct((points, lines), f32),
            jax.ShapeDtypeStruct((points, lines), f32),
            jax.ShapeDtypeStruct((2 * points, points), bf16),
            jax.ShapeDtypeStruct((5, points, LANES), f32),
            jax.ShapeDtypeStruct((2, tall, LANES), f32),
        ),
        in_specs=[hbm, hbm, hbm, hbm],
        out_specs=(vmem,) * 5,
        scratch_shapes=[
            pltpu.VMEM((peers, *eigvec.shape) if gathers else eigvec.shape, f32),
            pltpu.VMEM((1, points), f32),
            pltpu.VMEM(wavenumbers.shape, jnp.int32),
            pltpu.VMEM((points, lines), f32),
            pltpu.VMEM((points, lines), bf16),
            pltpu.VMEM((points, lines), bf16),
            pltpu.VMEM((peers if gathers else 1, rows, padded), f32),
            pltpu.VMEM((points, padded), f32),
            pltpu.VMEM((2 * points, points), bf16),
            pltpu.VMEM((3, tall, LANES), f32),
            pltpu.VMEM((groups, 3, tall, LANES), f32),
            pltpu.VMEM((2, tall, LANES), f32),
            pltpu.VMEM((groups, 2, tall, LANES), f32),
            dma((3,)),
            dma((chunks,)),
            dma((peers,)),
            dma((peers,)),
            dma((groups,)),
            dma((groups,)),
            dma((groups,)),
            dma((groups,)),
        ],
        compiler_params=pltpu.CompilerParams(
            collective_id=0, has_side_effects=True, vmem_limit_bytes=32 * 1024 * 1024
        ),
        name="helmholtz",
    )(*[
        pltpu.with_memory_space_constraint(operand, pltpu.HBM)
        for operand in (forcing, wavenumbers, eigvec, decay.reshape(1, points))
    ])
    return pl.pallas_call(
        finish,
        out_shape=jax.ShapeDtypeStruct((points, lines), f32),
        in_specs=[vmem] * 5,
        out_specs=hbm,
        scratch_shapes=[pltpu.VMEM((points, lines), f32), dma((chunks,))],
        compiler_params=pltpu.CompilerParams(vmem_limit_bytes=16 * 1024 * 1024),
        name="finish",
    )(*solved)


def solution(mesh):
    placed = (P("gy", "modes"), P(None, "modes"), P("gy", "modes"), P("gy"))
    return jax.shard_map(
        functools.partial(local, mesh.shape["modes"], mesh.shape["gy"]),
        mesh=mesh, in_specs=placed, out_specs=P("gy", "modes"), check_vma=False,
    )
```

```python
import functools

import jax
import jax.numpy as jnp
from jax import lax
from jax.experimental import pallas as pl
from jax.experimental.pallas import tpu as pltpu
from jax.sharding import PartitionSpec as P

coupling = 0.25
MESH = pl.DeviceIdType.MESH
LANES = 128
WIDE = 256


def split(value):
    high = value.astype(jnp.bfloat16)
    low = (value - high.astype(jnp.float32)).astype(jnp.bfloat16)
    return high, low


def product(stack, right_high, right_low):
    rows = stack.shape[0] // 2
    both = jnp.dot(stack[...], right_high, preferred_element_type=jnp.float32)
    last = jnp.dot(stack[:rows, :], right_low, preferred_element_type=jnp.float32)
    return both[:rows] + both[rows:] + last


def corner_states(corners):
    q_prev = jnp.zeros_like(corners[0][0])
    states = []
    for g_ss, g_se, g_ee in corners:
        scale = 1.0 / (1.0 - coupling * g_ss * q_prev)
        q_zero = coupling * g_se * scale
        q_one = coupling * g_ee + coupling * g_se * q_prev * q_zero
        states.append((scale, coupling * g_ss, coupling * g_se, coupling * g_se * q_prev, q_zero, q_one))
        q_prev = q_one
    return states


def neighbour_values(states, edge_values, here):
    groups = len(states)
    zero = jnp.zeros_like(edge_values[0][0])
    y_prev = zero
    values = []
    for (p_start, p_end), (scale, c_ss, c_se, c_seq, _, _) in zip(edge_values, states):
        zero_part = (p_start - c_ss * y_prev) * scale
        one_part = p_end - c_se * y_prev + c_seq * zero_part
        values.append((zero_part, one_part))
        y_prev = one_part
    a_next = mine_a = mine_b = zero
    for block in range(groups - 1, -1, -1):
        zero_part, one_part = values[block]
        q_zero, q_one = states[block][4:]
        mine_a = jnp.where(here == block, a_next, mine_a)
        if block < groups - 1:
            mine_b = jnp.where(here == block + 1, one_part - q_one * a_next, mine_b)
        a_next = zero_part - q_zero * a_next
    return mine_a, mine_b


def send_all(count, axis, src, dst, send_sem, recv_sem):
    me = lax.axis_index(axis)
    copies = []
    for step in range(1, count):
        peer = lax.rem(me + step, count)
        copy = pltpu.make_async_remote_copy(
            src_ref=src,
            dst_ref=dst(me),
            send_sem=send_sem.at[step],
            recv_sem=recv_sem.at[step],
            device_id={axis: peer},
            device_id_type=MESH,
        )
        copy.start()
        copies.append(copy)
    return copies


def inverse(value):
    near = pl.reciprocal(value, approx=True)
    return near * (2.0 - value * near)


def kernel(
    gathers, peers, groups,
    forcing, wavenumbers, eigvec, decay,
    weight, trans, stack, rows_bc, edges,
    flat, dec, numbers, f_buf, f_high, f_low, mine, matrix,
    stack_t, g_mine, g_all, p_mine, p_all,
    in_sem, f_sem, v_send, v_recv, g_send, g_recv, p_send, p_recv,
):
    points, lines = f_buf.shape
    chunks = lines // WIDE
    me = lax.axis_index("modes")
    here = lax.axis_index("gy")

    barrier = pltpu.get_barrier_semaphore()
    greeted = 0
    if gathers:
        for step in range(1, peers):
            pl.semaphore_signal(
                barrier, inc=1, device_id={"modes": lax.rem(me + step, peers)}, device_id_type=MESH
            )
        greeted = peers - 1
    for step in range(1, groups):
        pl.semaphore_signal(
            barrier, inc=1, device_id={"gy": lax.rem(here + step, groups)}, device_id_type=MESH
        )
    eig_load = pltpu.make_async_copy(eigvec, flat.at[0] if gathers else flat, in_sem.at[0])
    eig_load.start()
    dec_load = pltpu.make_async_copy(decay, dec, in_sem.at[1])
    dec_load.start()
    num_load = pltpu.make_async_copy(wavenumbers, numbers, in_sem.at[2])
    num_load.start()
    loads = []
    for chunk in range(chunks):
        cols = pl.ds(chunk * WIDE, WIDE)
        load = pltpu.make_async_copy(forcing.at[:, cols], f_buf.at[:, cols], f_sem.at[chunk])
        load.start()
        loads.append(load)

    rows = mine.shape[1]

    def unpack(place, block):
        line = flat[place]
        for row in range(rows):
            mine[place, row:row + 1, :points] = line[:, row * points:(row + 1) * points]
        matrix[pl.ds(pl.multiple_of(block * rows, 8), rows), :] = mine[place]

    hops = []
    if gathers:
        eig_load.wait()
        pl.semaphore_wait(barrier, greeted + groups - 1)
        for step in sorted(range(1, peers), key=lambda at: abs(2 * at - peers)):
            copy = pltpu.make_async_remote_copy(
                src_ref=flat.at[0],
                dst_ref=flat.at[step],
                send_sem=v_send.at[step],
                recv_sem=v_recv.at[step],
                device_id={"modes": lax.rem(me + step, peers)},
                device_id_type=MESH,
            )
            copy.start()
            hops.append((step, copy))
        unpack(0, me)
    else:
        pl.semaphore_wait(barrier, groups - 1)
        eig_load.wait()
        matrix[:, :points] = flat[...]

    dec_load.wait()
    num_load.wait()
    row_at = lax.broadcasted_iota(jnp.int32, (points, points), 0)
    col_at = lax.broadcasted_iota(jnp.int32, (points, points), 1)
    rate = jnp.sum(jnp.where(row_at == col_at, dec[...], 0.0), axis=1, keepdims=True)
    rate = jnp.broadcast_to(rate, (points, LANES))
    for chunk in range(lines // LANES):
        cols = slice(chunk * LANES, (chunk + 1) * LANES)
        kx = numbers[0:1, cols].astype(jnp.float32) / 64.0
        kz = numbers[1:2, cols].astype(jnp.float32) / 24.0
        weight[:, cols] = inverse(kx * kx + kz * kz + rate)
    for chunk in range(chunks):
        cols = slice(chunk * WIDE, (chunk + 1) * WIDE)
        loads[chunk].wait()
        f_high[:, cols], f_low[:, cols] = split(f_buf[:, cols])
    for step, copy in hops:
        copy.wait_recv()
        unpack(step, lax.rem(me + peers - step, peers))
    full = matrix[:, :points]
    stack[:points, :], stack[points:, :] = split(full)
    turned = full.T
    stack_t[:points, :], stack_t[points:, :] = split(turned)
    first = jnp.broadcast_to(turned[:, 0:1], (points, LANES))
    last = jnp.broadcast_to(turned[:, points - 1:points], (points, LANES))
    rows_bc[0] = first
    rows_bc[1] = last
    rows_bc[2] = first * first
    rows_bc[3] = first * last
    rows_bc[4] = last * last

    per = WIDE // LANES
    g_copies = []
    for chunk in range(chunks):
        cols = slice(chunk * WIDE, (chunk + 1) * WIDE)
        if 2 * chunk < chunks:
            for row in range(2 * chunk * per, min(2 * chunk + 2, chunks) * per):
                part = weight[:, row * LANES:(row + 1) * LANES]
                for which in range(3):
                    g_mine[which, row:row + 1, :] = jnp.sum(
                        rows_bc[2 + which] * part, axis=0, keepdims=True
                    )
            if 2 * chunk + 2 >= chunks:
                g_copies = send_all(groups, "gy", g_mine, lambda at: g_all.at[at], g_send, g_recv)
                g_all[here] = g_mine[...]
        value = product(stack_t, f_high[:, cols], f_low[:, cols])
        trans[:, cols] = value
        scaled = value * weight[:, cols]
        for half in range(WIDE // LANES):
            part = scaled[:, half * LANES:(half + 1) * LANES]
            row = chunk * (WIDE // LANES) + half
            for which in range(2):
                p_mine[which, row:row + 1, :] = jnp.sum(rows_bc[which] * part, axis=0, keepdims=True)
    p_copies = send_all(groups, "gy", p_mine, lambda at: p_all.at[at], p_send, p_recv)
    p_all[here] = p_mine[...]

    for copy in g_copies:
        copy.wait_recv()
    states = corner_states(
        [(g_all[block, 0], g_all[block, 1], g_all[block, 2]) for block in range(groups)]
    )
    for copy in p_copies:
        copy.wait_recv()
    a_next, b_prev = neighbour_values(
        states, [(p_all[block, 0], p_all[block, 1]) for block in range(groups)], here
    )
    edges[0] = coupling * a_next
    edges[1] = coupling * b_prev
    for copy in [copy for _, copy in hops] + g_copies + p_copies:
        copy.wait_send()


def finish(weight, trans, stack, rows_bc, edges, out, result, sem):
    points, lines = trans.shape
    stores = []
    for chunk in range(lines // WIDE):
        halves = []
        for half in range(WIDE // LANES):
            row = chunk * (WIDE // LANES) + half
            lane = slice(row * LANES, (row + 1) * LANES)
            bare = (
                trans[:, lane]
                - edges[0, row:row + 1, :] * rows_bc[1]
                - edges[1, row:row + 1, :] * rows_bc[0]
            )
            halves.append(weight[:, lane] * bare)
        high, low = split(jnp.concatenate(halves, axis=1))
        span = pl.ds(chunk * WIDE, WIDE)
        result[:, span] = product(stack, high, low)
        store = pltpu.make_async_copy(result.at[:, span], out.at[:, span], sem.at[chunk])
        store.start()
        stores.append(store)
    for store in stores:
        store.wait()


def local(peers, groups, forcing, wavenumbers, eigvec, decay):
    points, lines = forcing.shape
    held = eigvec.shape[1]
    gathers = held % (8 * points) == 0
    if not gathers:
        eigvec = lax.all_gather(eigvec, "modes", axis=1, tiled=True).reshape(points, points)
    rows = held // points if gathers else 8
    f32, bf16 = jnp.float32, jnp.bfloat16
    tall = lines // LANES
    padded = -(-points // LANES) * LANES
    chunks = lines // WIDE
    dma = pltpu.SemaphoreType.DMA
    vmem = pl.BlockSpec(memory_space=pltpu.VMEM)
    hbm = pl.BlockSpec(memory_space=pltpu.HBM)
    solved = pl.pallas_call(
        functools.partial(kernel, gathers, peers, groups),
        out_shape=(
            jax.ShapeDtypeStruct((points, lines), f32),
            jax.ShapeDtypeStruct((points, lines), f32),
            jax.ShapeDtypeStruct((2 * points, points), bf16),
            jax.ShapeDtypeStruct((5, points, LANES), f32),
            jax.ShapeDtypeStruct((2, tall, LANES), f32),
        ),
        in_specs=[hbm, hbm, hbm, hbm],
        out_specs=(vmem,) * 5,
        scratch_shapes=[
            pltpu.VMEM((peers, *eigvec.shape) if gathers else eigvec.shape, f32),
            pltpu.VMEM((1, points), f32),
            pltpu.VMEM(wavenumbers.shape, jnp.int32),
            pltpu.VMEM((points, lines), f32),
            pltpu.VMEM((points, lines), bf16),
            pltpu.VMEM((points, lines), bf16),
            pltpu.VMEM((peers if gathers else 1, rows, padded), f32),
            pltpu.VMEM((points, padded), f32),
            pltpu.VMEM((2 * points, points), bf16),
            pltpu.VMEM((3, tall, LANES), f32),
            pltpu.VMEM((groups, 3, tall, LANES), f32),
            pltpu.VMEM((2, tall, LANES), f32),
            pltpu.VMEM((groups, 2, tall, LANES), f32),
            dma((3,)),
            dma((chunks,)),
            dma((peers,)),
            dma((peers,)),
            dma((groups,)),
            dma((groups,)),
            dma((groups,)),
            dma((groups,)),
        ],
        compiler_params=pltpu.CompilerParams(
            collective_id=0, has_side_effects=True, vmem_limit_bytes=32 * 1024 * 1024
        ),
        name="helmholtz",
    )(*[
        pltpu.with_memory_space_constraint(operand, pltpu.HBM)
        for operand in (forcing, wavenumbers, eigvec, decay.reshape(1, points))
    ])
    return pl.pallas_call(
        finish,
        out_shape=jax.ShapeDtypeStruct((points, lines), f32),
        in_specs=[vmem] * 5,
        out_specs=hbm,
        scratch_shapes=[pltpu.VMEM((points, lines), f32), dma((chunks,))],
        compiler_params=pltpu.CompilerParams(vmem_limit_bytes=16 * 1024 * 1024),
        name="finish",
    )(*solved)


def solution(mesh):
    placed = (P("gy", "modes"), P(None, "modes"), P("gy", "modes"), P("gy"))
    return jax.shard_map(
        functools.partial(local, mesh.shape["modes"], mesh.shape["gy"]),
        mesh=mesh, in_specs=placed, out_specs=P("gy", "modes"), check_vma=False,
    )
```

```python
import functools

import jax
import jax.numpy as jnp
from jax import lax
from jax.experimental import pallas as pl
from jax.experimental.pallas import tpu as pltpu
from jax.sharding import PartitionSpec as P

coupling = 0.25
MESH = pl.DeviceIdType.MESH
LANES = 128
WIDE = 256


def split(value):
    high = value.astype(jnp.bfloat16)
    low = (value - high.astype(jnp.float32)).astype(jnp.bfloat16)
    return high, low


def product(stack, right_high, right_low):
    rows = stack.shape[0] // 2
    both = jnp.dot(stack[...], right_high, preferred_element_type=jnp.float32)
    last = jnp.dot(stack[:rows, :], right_low, preferred_element_type=jnp.float32)
    return both[:rows] + both[rows:] + last


def corner_states(corners):
    q_prev = jnp.zeros_like(corners[0][0])
    states = []
    for g_ss, g_se, g_ee in corners:
        scale = 1.0 / (1.0 - coupling * g_ss * q_prev)
        q_zero = coupling * g_se * scale
        q_one = coupling * g_ee + coupling * g_se * q_prev * q_zero
        states.append((scale, coupling * g_ss, coupling * g_se, coupling * g_se * q_prev, q_zero, q_one))
        q_prev = q_one
    return states


def neighbour_values(states, edge_values, here):
    groups = len(states)
    zero = jnp.zeros_like(edge_values[0][0])
    y_prev = zero
    values = []
    for (p_start, p_end), (scale, c_ss, c_se, c_seq, _, _) in zip(edge_values, states):
        zero_part = (p_start - c_ss * y_prev) * scale
        one_part = p_end - c_se * y_prev + c_seq * zero_part
        values.append((zero_part, one_part))
        y_prev = one_part
    a_next = mine_a = mine_b = zero
    for block in range(groups - 1, -1, -1):
        zero_part, one_part = values[block]
        q_zero, q_one = states[block][4:]
        mine_a = jnp.where(here == block, a_next, mine_a)
        if block < groups - 1:
            mine_b = jnp.where(here == block + 1, one_part - q_one * a_next, mine_b)
        a_next = zero_part - q_zero * a_next
    return mine_a, mine_b


def send_all(count, axis, src, dst, send_sem, recv_sem):
    me = lax.axis_index(axis)
    copies = []
    for step in range(1, count):
        peer = lax.rem(me + step, count)
        copy = pltpu.make_async_remote_copy(
            src_ref=src,
            dst_ref=dst(me),
            send_sem=send_sem.at[step],
            recv_sem=recv_sem.at[step],
            device_id={axis: peer},
            device_id_type=MESH,
        )
        copy.start()
        copies.append(copy)
    return copies


def inverse(value):
    near = pl.reciprocal(value, approx=True)
    return near * (2.0 - value * near)


def kernel(
    gathers, peers, groups,
    forcing, wavenumbers, eigvec, decay,
    weight, trans, stack, rows_bc, edges,
    flat, dec, numbers, f_buf, f_high, f_low, mine, matrix,
    stack_t, g_mine, g_all, p_mine, p_all,
    in_sem, f_sem, v_send, v_recv, g_send, g_recv, p_send, p_recv,
):
    points, lines = f_buf.shape
    chunks = lines // WIDE
    me = lax.axis_index("modes")
    here = lax.axis_index("gy")

    barrier = pltpu.get_barrier_semaphore()
    greeted = 0
    if gathers:
        for step in range(1, peers):
            pl.semaphore_signal(
                barrier, inc=1, device_id={"modes": lax.rem(me + step, peers)}, device_id_type=MESH
            )
        greeted = peers - 1
    for step in range(1, groups):
        pl.semaphore_signal(
            barrier, inc=1, device_id={"gy": lax.rem(here + step, groups)}, device_id_type=MESH
        )
    eig_load = pltpu.make_async_copy(eigvec, flat.at[0] if gathers else flat, in_sem.at[0])
    eig_load.start()
    dec_load = pltpu.make_async_copy(decay, dec, in_sem.at[1])
    dec_load.start()
    num_load = pltpu.make_async_copy(wavenumbers, numbers, in_sem.at[2])
    num_load.start()
    loads = []
    for chunk in range(chunks):
        cols = pl.ds(chunk * WIDE, WIDE)
        load = pltpu.make_async_copy(forcing.at[:, cols], f_buf.at[:, cols], f_sem.at[chunk])
        load.start()
        loads.append(load)

    rows = mine.shape[1]

    def unpack(place, block):
        line = flat[place]
        for row in range(rows):
            mine[place, row:row + 1, :points] = line[:, row * points:(row + 1) * points]
        matrix[pl.ds(pl.multiple_of(block * rows, 8), rows), :] = mine[place]

    hops = []
    if gathers:
        eig_load.wait()
        pl.semaphore_wait(barrier, greeted + groups - 1)
        for step in range(1, peers):
            copy = pltpu.make_async_remote_copy(
                src_ref=flat.at[0],
                dst_ref=flat.at[step],
                send_sem=v_send.at[step],
                recv_sem=v_recv.at[step],
                device_id={"modes": lax.rem(me + step, peers)},
                device_id_type=MESH,
            )
            copy.start()
            hops.append((step, copy))
        unpack(0, me)
    else:
        pl.semaphore_wait(barrier, groups - 1)
        eig_load.wait()
        matrix[:, :points] = flat[...]

    dec_load.wait()
    num_load.wait()
    row_at = lax.broadcasted_iota(jnp.int32, (points, points), 0)
    col_at = lax.broadcasted_iota(jnp.int32, (points, points), 1)
    rate = jnp.sum(jnp.where(row_at == col_at, dec[...], 0.0), axis=1, keepdims=True)
    rate = jnp.broadcast_to(rate, (points, LANES))
    for chunk in range(lines // LANES):
        cols = slice(chunk * LANES, (chunk + 1) * LANES)
        kx = numbers[0:1, cols].astype(jnp.float32) / 64.0
        kz = numbers[1:2, cols].astype(jnp.float32) / 24.0
        weight[:, cols] = inverse(kx * kx + kz * kz + rate)
    for chunk in range(chunks):
        cols = slice(chunk * WIDE, (chunk + 1) * WIDE)
        loads[chunk].wait()
        f_high[:, cols], f_low[:, cols] = split(f_buf[:, cols])
    for step, copy in hops:
        copy.wait_recv()
        unpack(step, lax.rem(me + peers - step, peers))
    full = matrix[:, :points]
    stack[:points, :], stack[points:, :] = split(full)
    turned = full.T
    stack_t[:points, :], stack_t[points:, :] = split(turned)
    first = jnp.broadcast_to(turned[:, 0:1], (points, LANES))
    last = jnp.broadcast_to(turned[:, points - 1:points], (points, LANES))
    rows_bc[0] = first
    rows_bc[1] = last
    rows_bc[2] = first * first
    rows_bc[3] = first * last
    rows_bc[4] = last * last

    per = WIDE // LANES
    g_copies = []
    for chunk in range(chunks):
        cols = slice(chunk * WIDE, (chunk + 1) * WIDE)
        if 2 * chunk < chunks:
            for row in range(2 * chunk * per, min(2 * chunk + 2, chunks) * per):
                part = weight[:, row * LANES:(row + 1) * LANES]
                for which in range(3):
                    g_mine[which, row:row + 1, :] = jnp.sum(
                        rows_bc[2 + which] * part, axis=0, keepdims=True
                    )
            if 2 * chunk + 2 >= chunks:
                g_copies = send_all(groups, "gy", g_mine, lambda at: g_all.at[at], g_send, g_recv)
                g_all[here] = g_mine[...]
        value = product(stack_t, f_high[:, cols], f_low[:, cols])
        trans[:, cols] = value
        scaled = value * weight[:, cols]
        for half in range(WIDE // LANES):
            part = scaled[:, half * LANES:(half + 1) * LANES]
            row = chunk * (WIDE // LANES) + half
            for which in range(2):
                p_mine[which, row:row + 1, :] = jnp.sum(rows_bc[which] * part, axis=0, keepdims=True)
    p_copies = send_all(groups, "gy", p_mine, lambda at: p_all.at[at], p_send, p_recv)
    p_all[here] = p_mine[...]

    for copy in g_copies:
        copy.wait_recv()
    states = corner_states(
        [(g_all[block, 0], g_all[block, 1], g_all[block, 2]) for block in range(groups)]
    )
    for copy in p_copies:
        copy.wait_recv()
    a_next, b_prev = neighbour_values(
        states, [(p_all[block, 0], p_all[block, 1]) for block in range(groups)], here
    )
    edges[0] = coupling * a_next
    edges[1] = coupling * b_prev
    for copy in [copy for _, copy in hops] + g_copies + p_copies:
        copy.wait_send()


def finish(weight, trans, stack, rows_bc, edges, out, result, sem):
    points, lines = trans.shape
    stores = []
    for chunk in range(lines // WIDE):
        halves = []
        for half in range(WIDE // LANES):
            row = chunk * (WIDE // LANES) + half
            lane = slice(row * LANES, (row + 1) * LANES)
            bare = (
                trans[:, lane]
                - edges[0, row:row + 1, :] * rows_bc[1]
                - edges[1, row:row + 1, :] * rows_bc[0]
            )
            halves.append(weight[:, lane] * bare)
        high, low = split(jnp.concatenate(halves, axis=1))
        span = pl.ds(chunk * WIDE, WIDE)
        result[:, span] = product(stack, high, low)
        store = pltpu.make_async_copy(result.at[:, span], out.at[:, span], sem.at[chunk])
        store.start()
        stores.append(store)
    for store in stores:
        store.wait()


def local(peers, groups, forcing, wavenumbers, eigvec, decay):
    points, lines = forcing.shape
    held = eigvec.shape[1]
    gathers = held % (8 * points) == 0
    if not gathers:
        eigvec = lax.all_gather(eigvec, "modes", axis=1, tiled=True).reshape(points, points)
    rows = held // points if gathers else 8
    f32, bf16 = jnp.float32, jnp.bfloat16
    tall = lines // LANES
    padded = -(-points // LANES) * LANES
    chunks = lines // WIDE
    dma = pltpu.SemaphoreType.DMA
    vmem = pl.BlockSpec(memory_space=pltpu.VMEM)
    hbm = pl.BlockSpec(memory_space=pltpu.HBM)
    solved = pl.pallas_call(
        functools.partial(kernel, gathers, peers, groups),
        out_shape=(
            jax.ShapeDtypeStruct((points, lines), f32),
            jax.ShapeDtypeStruct((points, lines), f32),
            jax.ShapeDtypeStruct((2 * points, points), bf16),
            jax.ShapeDtypeStruct((5, points, LANES), f32),
            jax.ShapeDtypeStruct((2, tall, LANES), f32),
        ),
        in_specs=[hbm, hbm, hbm, hbm],
        out_specs=(vmem,) * 5,
        scratch_shapes=[
            pltpu.VMEM((peers, *eigvec.shape) if gathers else eigvec.shape, f32),
            pltpu.VMEM((1, points), f32),
            pltpu.VMEM(wavenumbers.shape, jnp.int32),
            pltpu.VMEM((points, lines), f32),
            pltpu.VMEM((points, lines), bf16),
            pltpu.VMEM((points, lines), bf16),
            pltpu.VMEM((peers if gathers else 1, rows, padded), f32),
            pltpu.VMEM((points, padded), f32),
            pltpu.VMEM((2 * points, points), bf16),
            pltpu.VMEM((3, tall, LANES), f32),
            pltpu.VMEM((groups, 3, tall, LANES), f32),
            pltpu.VMEM((2, tall, LANES), f32),
            pltpu.VMEM((groups, 2, tall, LANES), f32),
            dma((3,)),
            dma((chunks,)),
            dma((peers,)),
            dma((peers,)),
            dma((groups,)),
            dma((groups,)),
            dma((groups,)),
            dma((groups,)),
        ],
        compiler_params=pltpu.CompilerParams(
            collective_id=0, has_side_effects=True, vmem_limit_bytes=32 * 1024 * 1024
        ),
        name="helmholtz",
    )(*[
        pltpu.with_memory_space_constraint(operand, pltpu.HBM)
        for operand in (forcing, wavenumbers, eigvec, decay.reshape(1, points))
    ])
    return pl.pallas_call(
        finish,
        out_shape=jax.ShapeDtypeStruct((points, lines), f32),
        in_specs=[vmem] * 5,
        out_specs=hbm,
        scratch_shapes=[pltpu.VMEM((points, lines), f32), dma((chunks,))],
        compiler_params=pltpu.CompilerParams(vmem_limit_bytes=16 * 1024 * 1024),
        name="finish",
    )(*solved)


def solution(mesh):
    placed = (P("gy", "modes"), P(None, "modes"), P("gy", "modes"), P("gy"))
    return jax.shard_map(
        functools.partial(local, mesh.shape["modes"], mesh.shape["gy"]),
        mesh=mesh, in_specs=placed, out_specs=P("gy", "modes"), check_vma=False,
    )
```
